32 devices in a mesh: shot: 8 (over z, x), az: 4 (over y, core).
Axes of the slice: x: 2, y: 2, z: 4, core: 2. Of those that a mesh axis runs over, the one named last changes fastest.
Arguments:
- spectra: bfloat16 [4, 32, 4096, 128], P('az', None, 'shot'), may hold values from -6 to 6
- sampled_mask: int32 [4, 32, 16, 256], P('az', 'shot'), may hold values 0 or 1
- counts: int32 [4, 32], P('az', 'shot'), may hold values from 1 to 6, as said below
Outputs:
- blended: bfloat16 [4, 32, 2048, 128], P('az', None, 'shot')
The draws below stay inside these ranges and needn't reach their ends.
Inputs may be any that keep to these rules, and one draw needn't show every extreme that they name: `counts`: every draw holds a patch with 1 iteration and a patch with 6.
All inputs are finite; a program needn't handle non-finite values. No bound on the sum of `sampled_mask` on one device may be relied on, other than what follows from the above.
Results may differ from the reference program's by a relative error of at most 0.008.
Values may be sent and summed in bfloat16 or wider, within the bound.
A program may use at most 64 MiB of HBM per device.

```python
import jax
import jax.numpy as jnp
from jax import lax

SIDE = 16
FREQ = 64
MAXIT = 6
PATCH_DEV = 4
NAZ = 4
P_AZ = 32


def draw_counts(key, part):
    light = jax.random.randint(key, (NAZ * P_AZ,), 0, 2, dtype=jnp.int32)
    heavy = jax.random.randint(jax.random.fold_in(key, 3), (NAZ * P_AZ,), 2, MAXIT + 1, dtype=jnp.int32)
    base = jnp.where(light == 0, jnp.ones_like(heavy), heavy).reshape(NAZ, P_AZ)
    base = base.at[0, :PATCH_DEV].set(MAXIT).at[1, :PATCH_DEV].set(1)
    return base


def plant(entries, own_key, smallest, top_value):
    shape = entries.shape
    index_at = [jax.random.randint(jax.random.fold_in(own_key, axis), (), 0, shape[axis]) for axis in range(len(shape))]
    entries = entries.at[tuple(index_at)].set(smallest)
    longest = shape.index(max(shape))
    index_at[longest] = (index_at[longest] + 1) % shape[longest]
    return entries.at[tuple(index_at)].set(top_value)


def shard_levels(own_key, shape, split, low, high):
    def one(dim, parts):
        draws = jax.random.uniform(jax.random.fold_in(jax.random.fold_in(own_key, 6), dim), (parts,), jnp.float32, low / len(split), high / len(split))
        return jnp.repeat(jnp.exp(draws), shape[dim] // parts).reshape((-1,) + (1,) * (len(shape) - dim - 1))

    factor_of = one(*split[0])
    for cut in split[1:]:
        factor_of = factor_of * one(*cut)
    return factor_of


def normal_values(stream_key, shape, scale, reach, shards=(), kind=jnp.bfloat16):
    values = jax.random.normal(stream_key, shape, jnp.float32) * scale
    if len(shards) > 0:
        values = shard_levels(stream_key, shape, shards, -0.22, 0.18) * values
    return jnp.clip(values, min=-reach, max=reach).astype(kind)


def setup_inputs(seed: int = 0) -> dict:
    seeds = jax.random.split(jax.random.key(seed), 4)
    spectra = normal_values(seeds[0], (NAZ, P_AZ, SIDE**3, 2 * FREQ), 1.0, 6.0, ((0, 4), (2, 8)))
    sampled_mask = plant((jax.random.randint(seeds[1], (NAZ, P_AZ, SIDE, SIDE * SIDE), 0, 2) < 1).astype(jnp.int32), jax.random.fold_in(seeds[1], 1), 0, 1)
    counts = draw_counts(jax.random.fold_in(seeds[3], 71), 0)
    return {"spectra": spectra, "sampled_mask": sampled_mask, "counts": counts}


def dft_tables(extent):
    indices = jnp.arange(extent, dtype=jnp.int32)
    product = indices[:, None] * indices[None, :] % extent
    phase = product.astype(jnp.float32) * (2.0 * jnp.pi / extent)
    scale = extent ** (-0.5)
    cos_table = jnp.cos(phase) * scale
    sin_table = -jnp.sin(phase) * scale
    kron_real = jnp.kron(cos_table, cos_table) - jnp.kron(sin_table, sin_table)
    kron_imag = jnp.kron(cos_table, sin_table) + jnp.kron(sin_table, cos_table)
    return (cos_table.astype(jnp.bfloat16), sin_table.astype(jnp.bfloat16), kron_real.astype(jnp.bfloat16), kron_imag.astype(jnp.bfloat16))

def apply_along(mat_real, mat_imag, volume, pattern):
    halfway = volume.shape[-1] // 2
    rotated = jnp.concatenate([-volume[..., halfway:], volume[..., :halfway]], axis=-1)
    first_part = jnp.einsum(pattern, mat_real.astype(jnp.float32), volume.astype(jnp.float32), precision=lax.Precision.HIGHEST)
    second_part = jnp.einsum(pattern, mat_imag.astype(jnp.float32), rotated.astype(jnp.float32), precision=lax.Precision.HIGHEST)
    return first_part + second_part

def project_patch(observed, mask_item, sweeps, tables):
    cos_table, sin_table, kron_real, kron_imag = tables
    sampled = (mask_item > 0)[:, :, None]
    initial = jnp.where(sampled, observed, jnp.zeros_like(observed)).astype(jnp.bfloat16)
    halfway = observed.shape[-1] // 2

    def forward(volume):
        middle = apply_along(kron_real, kron_imag, volume, 'kj,ajl->akl').astype(jnp.bfloat16)
        return apply_along(cos_table, sin_table, middle, 'ka,ajl->kjl')

    def inverse(volume):
        middle = apply_along(cos_table, -sin_table, volume, 'ka,ajl->kjl').astype(jnp.bfloat16)
        return apply_along(kron_real, -kron_imag, middle, 'kj,ajl->akl')

    def magnitude(coeffs):
        return jnp.sqrt(coeffs[..., :halfway] ** 2 + coeffs[..., halfway:] ** 2)
    largest = lax.optimization_barrier(jnp.max(magnitude(forward(initial)), axis=(0, 1)))

    def sweep_step(sweep, volume):
        coeffs = forward(volume)
        size_now = magnitude(coeffs)
        cutoff = largest * (0.5 * jnp.power(jnp.float32(0.6), sweep.astype(jnp.float32)))
        factor = jax.nn.relu(size_now - cutoff) / (jnp.maximum(size_now, cutoff) + 1e-06)
        thinned = (coeffs * jnp.concatenate([factor, factor], axis=-1)).astype(jnp.bfloat16)
        returned = inverse(thinned)
        return jnp.where(sampled, observed.astype(jnp.float32), returned).astype(jnp.bfloat16)
    return lax.fori_loop(0, sweeps, sweep_step, initial)

def reference(spectra, sampled_mask, counts):
    tables = dft_tables(SIDE)
    lane_count = 2 * FREQ
    patches = spectra.reshape(NAZ * P_AZ, SIDE, SIDE * SIDE, lane_count)
    masks = sampled_mask.reshape(NAZ * P_AZ, SIDE, SIDE * SIDE)
    sweeps = counts.reshape(NAZ * P_AZ)

    def run_patch(item):
        return project_patch(item[0], item[1], item[2], tables)
    result = lax.map(run_patch, (patches, masks, sweeps))
    result = result.reshape(NAZ, P_AZ, SIDE, SIDE * SIDE, lane_count)
    halfway = SIDE // 2
    own_half = result[:, :, :halfway].astype(jnp.float32)
    top_half = result[:, :, halfway:].astype(jnp.float32)
    earlier = jnp.concatenate([jnp.zeros((NAZ, 1, halfway, SIDE * SIDE, lane_count), jnp.float32), top_half[:, :-1]], axis=1)
    weight = ((jnp.arange(halfway, dtype=jnp.float32) + 0.5) / halfway)[:, None, None]
    blended = (weight * own_half + (1.0 - weight) * earlier).astype(jnp.bfloat16)
    return blended.reshape(NAZ, P_AZ, halfway * SIDE * SIDE, lane_count)
```

```python
import functools

import jax
import jax.numpy as jnp
import ml_dtypes
import numpy as np
from jax import lax
from jax.experimental import pallas as pl
from jax.experimental.pallas import tpu as pltpu
from jax.sharding import PartitionSpec as P


def rounded(table):
    return table.astype(ml_dtypes.bfloat16)


def real_form(real, imag):
    return np.block([[real, -imag], [imag, real]])


def dft_blocks(extent):
    n = np.arange(extent)
    phase = ((n[:, None] * n[None, :]) % extent).astype(np.float32) * np.float32(2.0 * np.pi / extent)
    scale = np.float32(extent ** (-0.5))
    cos = (np.cos(phase) * scale).astype(np.float32)
    sin = (-np.sin(phase) * scale).astype(np.float32)
    kr = np.kron(cos, cos) - np.kron(sin, sin)
    ki = np.kron(cos, sin) + np.kron(sin, cos)
    cos, sin, kr, ki = (rounded(t).astype(np.float32) for t in (cos, sin, kr, ki))
    half, plane = extent // 2, extent * extent
    eye = np.eye(extent, dtype=np.float32)
    ks = lambda t, par: t.reshape(half, 2, extent, plane)[:, par].reshape(plane // 2, plane)[:, : plane // 2]
    out = []
    for par in (0, 1):
        out.append(real_form(ks(kr, par), ks(ki, par)))
    for par in (0, 1):
        out.append(real_form(ks(kr, par).T, -ks(ki, par).T))
    for par in (0, 1):
        out.append(np.kron(real_form(cos[par::2, :half], sin[par::2, :half]), eye))
    for par in (0, 1):
        out.append(np.kron(real_form(cos[par::2, :half].T, -sin[par::2, :half].T), eye))
    return rounded(np.stack(out))


def dot(a, b):
    return jnp.dot(a, b, preferred_element_type=jnp.float32)


def patch_pair_kernel(counts_ref, obs_ref, mask_ref, table_ref, out_ref, mid, mid2, held, free, top):
    extent = obs_ref.shape[1]
    plane = obs_ref.shape[2]
    half = extent // 2
    lanes = obs_ref.shape[3]
    freq = lanes // 2
    hp = plane // 2
    first = pl.program_id(0) * 2
    count0, count1 = counts_ref[first], counts_ref[first + 1]
    most = jnp.maximum(count0, count1)
    low_lane = lax.broadcasted_iota(jnp.int32, (plane, lanes), 1) < freq

    def to_mid(m, xe, xo):
        for par, x in ((0, xe), (1, xo)):
            y = dot(table_ref[par], x.astype(jnp.bfloat16))
            lo, hi = y[:, :lanes], y[:, lanes:]
            for sd, v in ((0, lo + hi), (1, lo - hi)):
                v = v.astype(jnp.bfloat16).reshape(2, half, extent, lanes)
                for c in (0, 1):
                    mid[:, sd, c, m, :, par * lanes : (par + 1) * lanes] = v[c]

    def halves(x):
        a, b, c, d = x[:hp], x[hp:plane], x[plane : plane + hp], x[plane + hp :]
        return jnp.concatenate([a + b, c + d], 0), jnp.concatenate([a - b, c - d], 0)

    def begin(m, carry):
        row = lax.broadcasted_iota(jnp.int32, (2 * extent, 2 * lanes), 0)
        lane = lax.broadcasted_iota(jnp.int32, (2 * extent, 2 * lanes), 1)
        wanted = m + jnp.where(lane >= lanes, half, 0) + jnp.where(lane % lanes >= freq, extent, 0)
        pick = jnp.where(row == wanted, 1.0, 0.0).astype(jnp.bfloat16)
        marks = mask_ref[...].reshape(2 * extent, plane)
        spread = lax.dot_general(marks, pick, (((0,), (0,)), ((), ())), preferred_element_type=jnp.float32)
        free[m] = 1.0 - spread
        parts = []
        for hi in (0, 1):
            p0 = obs_ref[0, m + hi * half].astype(jnp.float32)
            p1 = obs_ref[1, m + hi * half].astype(jnp.float32)
            re = jnp.where(low_lane, p0, pltpu.roll(p1, freq, 1))
            im = jnp.where(low_lane, pltpu.roll(p0, freq, 1), p1)
            s = spread[:, hi * lanes : (hi + 1) * lanes]
            parts.append(jnp.concatenate([jnp.where(s > 0, re, 0.0), jnp.where(s > 0, im, 0.0)], 0))
        x = jnp.concatenate(parts, 1)
        held[m] = x.astype(jnp.bfloat16)
        xe, xo = halves(x)
        to_mid(m, xe, xo)
        return carry

    lax.fori_loop(0, half, begin, 0)

    def coefs(k1, sd):
        return dot(table_ref[4 + sd], mid[k1, sd].reshape(plane, 2 * lanes))

    def peak(k1, best):
        for sd in (0, 1):
            c = coefs(k1, sd)
            size = c[:hp] * c[:hp] + c[hp:] * c[hp:]
            best = jnp.maximum(best, jnp.max(size.reshape(hp // 8, 8, 2 * lanes), axis=0))
        return best

    best = lax.fori_loop(0, half, peak, jnp.zeros((8, 2 * lanes), jnp.float32))
    best = jnp.max(best, axis=0, keepdims=True)
    best = jnp.sqrt(jnp.maximum(best[:, :lanes], best[:, lanes:]))
    top[...] = jnp.broadcast_to(jnp.concatenate([best, best], 1) * 0.5, top.shape)

    def shrink(k1, cutoff):
        back = []
        for sd in (0, 1):
            c = coefs(k1, sd)
            re, im = c[:hp], c[hp:]
            square = jnp.maximum(re * re + im * im, 1e-30)
            size = square * lax.rsqrt(square)
            factor = jnp.maximum(size - cutoff, 0.0) * pl.reciprocal(size + 1e-6, approx=True)
            thin = jnp.concatenate([(re * factor).astype(jnp.bfloat16), (im * factor).astype(jnp.bfloat16)], 0)
            back.append(dot(table_ref[6 + sd], thin))
        for ab, v in ((0, back[0] + back[1]), (1, back[0] - back[1])):
            v = v.astype(jnp.bfloat16).reshape(2, half, extent, 2 * lanes)
            for par in (0, 1):
                for c in (0, 1):
                    mid2[:, par, c, k1, :, ab * lanes : (ab + 1) * lanes] = v[c, :, :, par * lanes : (par + 1) * lanes]
        return cutoff

    def returned(m):
        e = dot(table_ref[2], mid2[m, 0].reshape(plane, 2 * lanes))
        o = dot(table_ref[3], mid2[m, 1].reshape(plane, 2 * lanes))
        s, d = e + o, e - o
        open_ = free[m]
        obs = held[m].astype(jnp.float32)
        re = obs[:plane] + open_ * jnp.concatenate([s[:hp], d[:hp]], 0)
        im = obs[plane:] + open_ * jnp.concatenate([s[hp:], d[hp:]], 0)
        return re, im

    def again(m, carry):
        re, im = returned(m)
        xe, xo = halves(jnp.concatenate([re, im], 0))
        to_mid(m, xe, xo)
        return carry

    def sweep(k, carry):
        cutoff = top[0:1]
        lax.fori_loop(0, half, shrink, cutoff)
        top[...] = top[...] * 0.6
        ends0, ends1 = k == count0 - 1, k == count1 - 1

        def give(m, carry):
            re, im = returned(m)
            for hi in (0, 1):
                r, i = re[:, hi * lanes : (hi + 1) * lanes], im[:, hi * lanes : (hi + 1) * lanes]

                @pl.when(ends0)
                def _():
                    out_ref[0, m + hi * half] = jnp.where(low_lane, r, pltpu.roll(i, freq, 1)).astype(jnp.bfloat16)

                @pl.when(ends1)
                def _():
                    out_ref[1, m + hi * half] = jnp.where(low_lane, pltpu.roll(r, freq, 1), i).astype(jnp.bfloat16)

            @pl.when(k < most - 1)
            def _():
                xe, xo = halves(jnp.concatenate([re, im], 0))
                to_mid(m, xe, xo)

            return carry

        @pl.when(ends0 | ends1)
        def _():
            lax.fori_loop(0, half, give, 0)

        @pl.when(jnp.logical_not(ends0 | ends1))
        def _():
            lax.fori_loop(0, half, again, 0)

        return carry

    lax.fori_loop(0, most, sweep, 0)


def project(observed, masks, sweeps):
    owned, extent, plane, lanes = observed.shape
    half = extent // 2
    tables = jnp.asarray(dft_blocks(extent))
    block = (2, extent, plane, lanes)
    return pl.pallas_call(
        patch_pair_kernel,
        grid=(owned // 2,),
        out_shape=jax.ShapeDtypeStruct(observed.shape, jnp.bfloat16),
        in_specs=[
            pl.BlockSpec(memory_space=pltpu.SMEM),
            pl.BlockSpec(block, lambda i: (i, 0, 0, 0)),
            pl.BlockSpec((2, extent, plane), lambda i: (i, 0, 0)),
            pl.BlockSpec(tables.shape, lambda i: (0, 0, 0)),
        ],
        out_specs=pl.BlockSpec(block, lambda i: (i, 0, 0, 0)),
        scratch_shapes=[
            pltpu.VMEM((half, 2, 2, half, extent, 2 * lanes), jnp.bfloat16),
            pltpu.VMEM((half, 2, 2, half, extent, 2 * lanes), jnp.bfloat16),
            pltpu.VMEM((half, 2 * plane, 2 * lanes), jnp.bfloat16),
            pltpu.VMEM((half, plane, 2 * lanes), jnp.float32),
            pltpu.VMEM((8, 2 * lanes), jnp.float32),
        ],
        compiler_params=pltpu.CompilerParams(vmem_limit_bytes=48 * 2**20),
        cost_estimate=pl.CostEstimate(flops=owned * 5 * 2**30, bytes_accessed=2**23, transcendentals=2**20),
    )(sweeps, observed, masks.astype(jnp.bfloat16), tables)


def passed_along(block, axis, distance):
    devices = range(lax.axis_size(axis))
    route = [(i - distance, i) for i in devices if i - distance in devices]
    return lax.ppermute(block, axis, route)


def shards(spectra, sampled_mask, counts):
    regrouped = lax.all_to_all(spectra, "shot", split_axis=1, concat_axis=2, tiled=True)
    owned = regrouped.shape[1]
    extent = sampled_mask.shape[2]
    plane = extent * extent
    lanes = regrouped.shape[3]
    observed = regrouped.reshape(owned, extent, plane, lanes)
    result = project(observed, sampled_mask[0], counts[0])
    half = extent // 2
    arrived = passed_along(result[-1, half:], "shot", 1)
    earlier = jnp.concatenate([arrived[None], result[:-1, half:]], axis=0).astype(jnp.float32)
    weight = ((jnp.arange(half, dtype=jnp.float32) + 0.5) / half)[:, None, None]
    mixed = weight * result[:, :half].astype(jnp.float32) + (1.0 - weight) * earlier
    mixed = mixed.astype(jnp.bfloat16).reshape(1, owned, half * plane, lanes)
    return lax.all_to_all(mixed, "shot", split_axis=2, concat_axis=1, tiled=True)


def solution(mesh):
    return jax.shard_map(
        shards,
        mesh=mesh,
        in_specs=(P("az", None, "shot", None), P("az", "shot", None, None), P("az", "shot")),
        out_specs=P("az", None, "shot", None),
        check_vma=False,
    )
```

```python
import functools

import jax
import jax.numpy as jnp
import ml_dtypes
import numpy as np
from jax import lax
from jax.experimental import pallas as pl
from jax.experimental.pallas import tpu as pltpu
from jax.sharding import PartitionSpec as P


def rounded(table):
    return table.astype(ml_dtypes.bfloat16)


def real_form(real, imag):
    return np.block([[real, -imag], [imag, real]])


def dft_blocks(extent):
    n = np.arange(extent)
    phase = ((n[:, None] * n[None, :]) % extent).astype(np.float32) * np.float32(2.0 * np.pi / extent)
    scale = np.float32(extent ** (-0.5))
    cos = (np.cos(phase) * scale).astype(np.float32)
    sin = (-np.sin(phase) * scale).astype(np.float32)
    kr = np.kron(cos, cos) - np.kron(sin, sin)
    ki = np.kron(cos, sin) + np.kron(sin, cos)
    cos, sin, kr, ki = (rounded(t).astype(np.float32) for t in (cos, sin, kr, ki))
    half, plane = extent // 2, extent * extent
    eye = np.eye(extent, dtype=np.float32)
    ks = lambda t, par: t.reshape(half, 2, extent, plane)[:, par].reshape(plane // 2, plane)[:, : plane // 2]
    out = []
    for par in (0, 1):
        out.append(real_form(ks(kr, par), ks(ki, par)))
    for par in (0, 1):
        out.append(real_form(ks(kr, par).T, -ks(ki, par).T))
    for par in (0, 1):
        out.append(np.kron(real_form(cos[par::2, :half], sin[par::2, :half]), eye))
    for par in (0, 1):
        out.append(np.kron(real_form(cos[par::2, :half].T, -sin[par::2, :half].T), eye))
    return rounded(np.stack(out))


def dot(a, b):
    return jnp.dot(a, b, preferred_element_type=jnp.float32)


def patch_pair_kernel(counts_ref, obs_ref, mask_ref, table_ref, out_ref, mid, mid2, held, free, top):
    extent, plane = mask_ref.shape[1:]
    rows = obs_ref.shape[2]
    half = extent // 2
    lanes = obs_ref.shape[3]
    freq = lanes // 2
    hp = plane // 2
    count0, count1 = counts_ref[0], counts_ref[1]
    most = jnp.maximum(count0, count1)
    low_lane = lax.broadcasted_iota(jnp.int32, (plane, lanes), 1) < freq

    def observed(p, a):
        if rows >= plane:
            per = rows // plane
            block = obs_ref[a // per, p, pl.ds(pl.multiple_of(a % per * plane, plane), plane)]
        else:
            per = plane // rows
            block = obs_ref[pl.ds(a * per, per), p].reshape(plane, lanes)
        return block.astype(jnp.float32)

    def to_mid(m, xe, xo):
        for par, x in ((0, xe), (1, xo)):
            y = dot(table_ref[par], x.astype(jnp.bfloat16))
            lo, hi = y[:, :lanes], y[:, lanes:]
            for sd, v in ((0, lo + hi), (1, lo - hi)):
                v = v.astype(jnp.bfloat16).reshape(2, half, extent, lanes)
                for c in (0, 1):
                    mid[:, sd, c, m, :, par * lanes : (par + 1) * lanes] = v[c]

    def halves(x):
        a, b, c, d = x[:hp], x[hp:plane], x[plane : plane + hp], x[plane + hp :]
        return jnp.concatenate([a + b, c + d], 0), jnp.concatenate([a - b, c - d], 0)

    def begin(m, carry):
        row = lax.broadcasted_iota(jnp.int32, (2 * extent, 2 * lanes), 0)
        lane = lax.broadcasted_iota(jnp.int32, (2 * extent, 2 * lanes), 1)
        wanted = m + jnp.where(lane >= lanes, half, 0) + jnp.where(lane % lanes >= freq, extent, 0)
        pick = jnp.where(row == wanted, 1.0, 0.0).astype(jnp.bfloat16)
        marks = mask_ref[...].reshape(2 * extent, plane)
        spread = lax.dot_general(marks, pick, (((0,), (0,)), ((), ())), preferred_element_type=jnp.float32)
        free[m] = 1.0 - spread
        parts = []
        for hi in (0, 1):
            p0 = observed(0, m + hi * half)
            p1 = observed(1, m + hi * half)
            re = jnp.where(low_lane, p0, pltpu.roll(p1, freq, 1))
            im = jnp.where(low_lane, pltpu.roll(p0, freq, 1), p1)
            s = spread[:, hi * lanes : (hi + 1) * lanes]
            parts.append(jnp.concatenate([jnp.where(s > 0, re, 0.0), jnp.where(s > 0, im, 0.0)], 0))
        x = jnp.concatenate(parts, 1)
        held[m] = x.astype(jnp.bfloat16)
        xe, xo = halves(x)
        to_mid(m, xe, xo)
        return carry

    lax.fori_loop(0, half, begin, 0, unroll=8)

    def coefs(k1, sd):
        return dot(table_ref[4 + sd], mid[k1, sd].reshape(plane, 2 * lanes))

    def peak(k1, best):
        for sd in (0, 1):
            c = coefs(k1, sd)
            size = c[:hp] * c[:hp] + c[hp:] * c[hp:]
            best = jnp.maximum(best, jnp.max(size.reshape(hp // 8, 8, 2 * lanes), axis=0))
        return best

    best = lax.fori_loop(0, half, peak, jnp.zeros((8, 2 * lanes), jnp.float32), unroll=8)
    best = jnp.max(best, axis=0, keepdims=True)
    best = jnp.sqrt(jnp.maximum(best[:, :lanes], best[:, lanes:]))
    top[...] = jnp.broadcast_to(jnp.concatenate([best, best], 1) * 0.5, top.shape)

    def shrink(k1, cutoff):
        back = []
        for sd in (0, 1):
            c = coefs(k1, sd)
            re, im = c[:hp], c[hp:]
            square = jnp.maximum(re * re + im * im, 1e-30)
            size = square * lax.rsqrt(square)
            factor = jnp.maximum(size - cutoff, 0.0) * pl.reciprocal(size + 1e-6, approx=True)
            thin = jnp.concatenate([(re * factor).astype(jnp.bfloat16), (im * factor).astype(jnp.bfloat16)], 0)
            back.append(dot(table_ref[6 + sd], thin))
        for ab, v in ((0, back[0] + back[1]), (1, back[0] - back[1])):
            v = v.astype(jnp.bfloat16).reshape(2, half, extent, 2 * lanes)
            for par in (0, 1):
                for c in (0, 1):
                    mid2[:, par, c, k1, :, ab * lanes : (ab + 1) * lanes] = v[c, :, :, par * lanes : (par + 1) * lanes]
        return cutoff

    def returned(m):
        e = dot(table_ref[2], mid2[m, 0].reshape(plane, 2 * lanes))
        o = dot(table_ref[3], mid2[m, 1].reshape(plane, 2 * lanes))
        s, d = e + o, e - o
        open_ = free[m]
        obs = held[m].astype(jnp.float32)
        re = obs[:plane] + open_ * jnp.concatenate([s[:hp], d[:hp]], 0)
        im = obs[plane:] + open_ * jnp.concatenate([s[hp:], d[hp:]], 0)
        return re, im

    def again(m, carry):
        re, im = returned(m)
        xe, xo = halves(jnp.concatenate([re, im], 0))
        to_mid(m, xe, xo)
        return carry

    def sweep(k, carry):
        cutoff = top[0:1]
        lax.fori_loop(0, half, shrink, cutoff, unroll=8)
        top[...] = top[...] * 0.6
        ends0, ends1 = k == count0 - 1, k == count1 - 1

        def give(m, carry):
            re, im = returned(m)
            for hi in (0, 1):
                r, i = re[:, hi * lanes : (hi + 1) * lanes], im[:, hi * lanes : (hi + 1) * lanes]

                @pl.when(ends0)
                def _():
                    out_ref[0, m + hi * half] = jnp.where(low_lane, r, pltpu.roll(i, freq, 1)).astype(jnp.bfloat16)

                @pl.when(ends1)
                def _():
                    out_ref[1, m + hi * half] = jnp.where(low_lane, pltpu.roll(r, freq, 1), i).astype(jnp.bfloat16)

            @pl.when(k < most - 1)
            def _():
                xe, xo = halves(jnp.concatenate([re, im], 0))
                to_mid(m, xe, xo)

            return carry

        @pl.when(ends0 | ends1)
        def _():
            lax.fori_loop(0, half, give, 0, unroll=8)

        @pl.when(jnp.logical_not(ends0 | ends1))
        def _():
            lax.fori_loop(0, half, again, 0, unroll=8)

        return carry

    lax.fori_loop(0, most, sweep, 0)


def project(received, masks, sweeps, tables):
    lanes = received.shape[3]
    extent, plane = masks.shape[1:]
    half = extent // 2
    whole = pl.BlockSpec(memory_space=pltpu.VMEM)
    return pl.pallas_call(
        patch_pair_kernel,
        out_shape=jax.ShapeDtypeStruct((2, extent, plane, lanes), jnp.bfloat16),
        in_specs=[pl.BlockSpec(memory_space=pltpu.SMEM), whole, whole, whole],
        out_specs=whole,
        scratch_shapes=[
            pltpu.VMEM((half, 2, 2, half, extent, 2 * lanes), jnp.bfloat16),
            pltpu.VMEM((half, 2, 2, half, extent, 2 * lanes), jnp.bfloat16),
            pltpu.VMEM((half, 2 * plane, 2 * lanes), jnp.bfloat16),
            pltpu.VMEM((half, plane, 2 * lanes), jnp.float32),
            pltpu.VMEM((8, 2 * lanes), jnp.float32),
        ],
        compiler_params=pltpu.CompilerParams(vmem_limit_bytes=40 * 2**20),
        cost_estimate=pl.CostEstimate(flops=40 * 2**30, bytes_accessed=2**23, transcendentals=2**20),
    )(sweeps, received, masks.astype(jnp.bfloat16), tables)


def passed_along(block, axis, distance):
    devices = range(lax.axis_size(axis))
    route = [(i - distance, i) for i in devices if i - distance in devices]
    return lax.ppermute(block, axis, route)


def exchanged(parts):
    return lax.all_to_all(parts, "shot", split_axis=0, concat_axis=0, tiled=True)


def shards(spectra, sampled_mask, counts):
    devices = lax.axis_size("shot")
    owned, extent, plane = sampled_mask.shape[1:]
    rows, lanes = spectra.shape[2:]
    half = extent // 2
    tables = jnp.asarray(dft_blocks(extent))
    by_owner = spectra.reshape(devices, owned, rows, lanes)
    starts = range(owned - 2, -1, -2)
    received = [exchanged(by_owner[:, s : s + 2]) for s in starts]
    weight = ((jnp.arange(half, dtype=jnp.float32) + 0.5) / half)[:, None, None]

    def blend(own, earlier):
        mixed = weight * own.astype(jnp.float32) + (1.0 - weight) * earlier.astype(jnp.float32)
        return mixed.astype(jnp.bfloat16).reshape(devices, half * plane // devices, lanes)

    lower = None
    for part, s in zip(received, starts):
        result = project(part, sampled_mask[0, s : s + 2], counts[0, s : s + 2], tables)
        if lower is None:
            arrived = passed_along(result[1, half:], "shot", 1)
            last = exchanged(blend(result[1, :half], result[0, half:]))[:, None]
            late = []
        else:
            late = [blend(result[1, :half], result[0, half:]), blend(lower, result[1, half:])] + late
        lower = result[0, :half]
    late = [blend(lower, arrived)] + late
    return jnp.concatenate([exchanged(jnp.stack(late, 1)), last], 1).reshape(1, devices * owned, half * plane // devices, lanes)


def solution(mesh):
    return jax.shard_map(
        shards,
        mesh=mesh,
        in_specs=(P("az", None, "shot", None), P("az", "shot", None, None), P("az", "shot")),
        out_specs=P("az", None, "shot", None),
        check_vma=False,
    )
```

```python
import functools

import jax
import jax.numpy as jnp
import ml_dtypes
import numpy as np
from jax import lax
from jax.experimental import pallas as pl
from jax.experimental.pallas import tpu as pltpu
from jax.sharding import PartitionSpec as P


def rounded(table):
    return table.astype(ml_dtypes.bfloat16)


def real_form(real, imag):
    return np.block([[real, -imag], [imag, real]])


def dft_blocks(extent):
    n = np.arange(extent)
    phase = ((n[:, None] * n[None, :]) % extent).astype(np.float32) * np.float32(2.0 * np.pi / extent)
    scale = np.float32(extent ** (-0.5))
    cos = (np.cos(phase) * scale).astype(np.float32)
    sin = (-np.sin(phase) * scale).astype(np.float32)
    kr = np.kron(cos, cos) - np.kron(sin, sin)
    ki = np.kron(cos, sin) + np.kron(sin, cos)
    cos, sin, kr, ki = (rounded(t).astype(np.float32) for t in (cos, sin, kr, ki))
    half, plane = extent // 2, extent * extent
    eye = np.eye(extent, dtype=np.float32)
    ks = lambda t, par: t.reshape(half, 2, extent, plane)[:, par].reshape(plane // 2, plane)[:, : plane // 2]
    out = []
    for par in (0, 1):
        out.append(real_form(ks(kr, par), ks(ki, par)))
    for par in (0, 1):
        out.append(real_form(ks(kr, par).T, -ks(ki, par).T))
    for par in (0, 1):
        out.append(np.kron(real_form(cos[par::2, :half], sin[par::2, :half]), eye))
    for par in (0, 1):
        out.append(np.kron(real_form(cos[par::2, :half].T, -sin[par::2, :half].T), eye))
    return rounded(np.stack(out))


def dot(a, b):
    return jnp.dot(a, b, preferred_element_type=jnp.float32)


def patch_pair_kernel(counts_ref, obs_ref, mask_ref, table_ref, out_ref, mid, mid2, held, free, top):
    extent, plane = mask_ref.shape[1:]
    rows = obs_ref.shape[2]
    half = extent // 2
    lanes = obs_ref.shape[3]
    freq = lanes // 2
    hp = plane // 2
    count0, count1 = counts_ref[0], counts_ref[1]
    most = jnp.maximum(count0, count1)
    low_lane = lax.broadcasted_iota(jnp.int32, (plane, lanes), 1) < freq

    def observed(p, a):
        if rows >= plane:
            per = rows // plane
            block = obs_ref[a // per, p, pl.ds(pl.multiple_of(a % per * plane, plane), plane)]
        else:
            per = plane // rows
            block = obs_ref[pl.ds(a * per, per), p].reshape(plane, lanes)
        return block.astype(jnp.float32)

    def to_mid(m, xe, xo):
        for par, x in ((0, xe), (1, xo)):
            y = dot(table_ref[par], x.astype(jnp.bfloat16))
            lo, hi = y[:, :lanes], y[:, lanes:]
            for sd, v in ((0, lo + hi), (1, lo - hi)):
                v = v.astype(jnp.bfloat16).reshape(2, half, extent, lanes)
                for c in (0, 1):
                    mid[:, sd, c, m, :, par * lanes : (par + 1) * lanes] = v[c]

    def halves(x):
        a, b, c, d = x[:hp], x[hp:plane], x[plane : plane + hp], x[plane + hp :]
        return jnp.concatenate([a + b, c + d], 0), jnp.concatenate([a - b, c - d], 0)

    def begin(m, carry):
        row = lax.broadcasted_iota(jnp.int32, (2 * extent, 2 * lanes), 0)
        lane = lax.broadcasted_iota(jnp.int32, (2 * extent, 2 * lanes), 1)
        wanted = m + jnp.where(lane >= lanes, half, 0) + jnp.where(lane % lanes >= freq, extent, 0)
        pick = jnp.where(row == wanted, 1.0, 0.0).astype(jnp.bfloat16)
        marks = mask_ref[...].reshape(2 * extent, plane)
        spread = lax.dot_general(marks, pick, (((0,), (0,)), ((), ())), preferred_element_type=jnp.float32)
        free[m] = 1.0 - spread
        parts = []
        for hi in (0, 1):
            p0 = observed(0, m + hi * half)
            p1 = observed(1, m + hi * half)
            re = jnp.where(low_lane, p0, pltpu.roll(p1, freq, 1))
            im = jnp.where(low_lane, pltpu.roll(p0, freq, 1), p1)
            s = spread[:, hi * lanes : (hi + 1) * lanes]
            parts.append(jnp.concatenate([jnp.where(s > 0, re, 0.0), jnp.where(s > 0, im, 0.0)], 0))
        x = jnp.concatenate(parts, 1)
        held[m] = x.astype(jnp.bfloat16)
        xe, xo = halves(x)
        to_mid(m, xe, xo)
        return carry

    lax.fori_loop(0, half, begin, 0, unroll=8)

    def coefs(k1, sd):
        return dot(table_ref[4 + sd], mid[k1, sd].reshape(plane, 2 * lanes))

    def peak(k1, best):
        for sd in (0, 1):
            c = coefs(k1, sd)
            size = c[:hp] * c[:hp] + c[hp:] * c[hp:]
            best = jnp.maximum(best, jnp.max(size.reshape(hp // 8, 8, 2 * lanes), axis=0))
        return best

    best = lax.fori_loop(0, half, peak, jnp.zeros((8, 2 * lanes), jnp.float32), unroll=8)
    best = jnp.max(best, axis=0, keepdims=True)
    best = jnp.sqrt(jnp.maximum(best[:, :lanes], best[:, lanes:]))
    top[...] = jnp.broadcast_to(jnp.concatenate([best, best], 1) * 0.5, top.shape)

    def shrink(k1, cutoff):
        back = []
        for sd in (0, 1):
            c = coefs(k1, sd)
            re, im = c[:hp], c[hp:]
            square = jnp.maximum(re * re + im * im, 1e-30)
            size = square * lax.rsqrt(square)
            factor = jnp.maximum(size - cutoff, 0.0) * pl.reciprocal(size + 1e-6, approx=True)
            thin = jnp.concatenate([(re * factor).astype(jnp.bfloat16), (im * factor).astype(jnp.bfloat16)], 0)
            back.append(dot(table_ref[6 + sd], thin))
        for ab, v in ((0, back[0] + back[1]), (1, back[0] - back[1])):
            v = v.astype(jnp.bfloat16).reshape(2, half, extent, 2 * lanes)
            for par in (0, 1):
                for c in (0, 1):
                    mid2[:, par, c, k1, :, ab * lanes : (ab + 1) * lanes] = v[c, :, :, par * lanes : (par + 1) * lanes]
        return cutoff

    def returned(m):
        e = dot(table_ref[2], mid2[m, 0].reshape(plane, 2 * lanes))
        o = dot(table_ref[3], mid2[m, 1].reshape(plane, 2 * lanes))
        s, d = e + o, e - o
        open_ = free[m]
        obs = held[m].astype(jnp.float32)
        re = obs[:plane] + open_ * jnp.concatenate([s[:hp], d[:hp]], 0)
        im = obs[plane:] + open_ * jnp.concatenate([s[hp:], d[hp:]], 0)
        return re, im

    def again(m, carry):
        re, im = returned(m)
        xe, xo = halves(jnp.concatenate([re, im], 0))
        to_mid(m, xe, xo)
        return carry

    def sweep(k, carry):
        cutoff = top[0:1]
        lax.fori_loop(0, half, shrink, cutoff, unroll=8)
        top[...] = top[...] * 0.6
        ends0, ends1 = k == count0 - 1, k == count1 - 1

        def give(m, carry):
            re, im = returned(m)
            for hi in (0, 1):
                r, i = re[:, hi * lanes : (hi + 1) * lanes], im[:, hi * lanes : (hi + 1) * lanes]

                @pl.when(ends0)
                def _():
                    out_ref[0, m + hi * half] = jnp.where(low_lane, r, pltpu.roll(i, freq, 1)).astype(jnp.bfloat16)

                @pl.when(ends1)
                def _():
                    out_ref[1, m + hi * half] = jnp.where(low_lane, pltpu.roll(r, freq, 1), i).astype(jnp.bfloat16)

            @pl.when(k < most - 1)
            def _():
                xe, xo = halves(jnp.concatenate([re, im], 0))
                to_mid(m, xe, xo)

            return carry

        @pl.when(ends0 | ends1)
        def _():
            lax.fori_loop(0, half, give, 0, unroll=8)

        @pl.when(jnp.logical_not(ends0 | ends1))
        def _():
            lax.fori_loop(0, half, again, 0, unroll=8)

        return carry

    lax.fori_loop(0, most, sweep, 0)


def project(received, masks, sweeps, tables):
    lanes = received.shape[3]
    extent, plane = masks.shape[1:]
    half = extent // 2
    whole = pl.BlockSpec(memory_space=pltpu.VMEM)
    return pl.pallas_call(
        patch_pair_kernel,
        out_shape=jax.ShapeDtypeStruct((2, extent, plane, lanes), jnp.bfloat16),
        in_specs=[pl.BlockSpec(memory_space=pltpu.SMEM), whole, whole, whole],
        out_specs=whole,
        scratch_shapes=[
            pltpu.VMEM((half, 2, 2, half, extent, 2 * lanes), jnp.bfloat16),
            pltpu.VMEM((half, 2, 2, half, extent, 2 * lanes), jnp.bfloat16),
            pltpu.VMEM((half, 2 * plane, 2 * lanes), jnp.bfloat16),
            pltpu.VMEM((half, plane, 2 * lanes), jnp.float32),
            pltpu.VMEM((8, 2 * lanes), jnp.float32),
        ],
        compiler_params=pltpu.CompilerParams(vmem_limit_bytes=40 * 2**20),
        cost_estimate=pl.CostEstimate(flops=40 * 2**30, bytes_accessed=2**23, transcendentals=2**20),
    )(sweeps, received, masks.astype(jnp.bfloat16), tables)


def passed_along(block, axis, distance):
    devices = range(lax.axis_size(axis))
    route = [(i - distance, i) for i in devices if i - distance in devices]
    return lax.ppermute(block, axis, route)


def exchanged(parts):
    return lax.all_to_all(parts, "shot", split_axis=0, concat_axis=0, tiled=True)


def shards(spectra, sampled_mask, counts):
    devices = lax.axis_size("shot")
    owned, extent, plane = sampled_mask.shape[1:]
    rows, lanes = spectra.shape[2:]
    half = extent // 2
    tables = jnp.asarray(dft_blocks(extent))
    by_owner = spectra.reshape(devices, owned, rows, lanes)
    starts = range(owned - 2, -1, -2)
    received = [exchanged(by_owner[:, s : s + 2]) for s in starts]
    weight = ((jnp.arange(half, dtype=jnp.float32) + 0.5) / half)[:, None, None]

    def blend(own, earlier):
        mixed = weight * own.astype(jnp.float32) + (1.0 - weight) * earlier.astype(jnp.float32)
        return mixed.astype(jnp.bfloat16).reshape(devices, half * plane // devices, lanes)

    lower = None
    for i, s in enumerate(starts):
        part = received[i]
        result = project(part, sampled_mask[0, s : s + 2], counts[0, s : s + 2], tables)
        if lower is None:
            arrived = passed_along(result[1, half:], "shot", 1)
            first = blend(result[1, :half], result[0, half:])
            if len(received) > 1:
                first, received[1] = lax.optimization_barrier((first, received[1]))
            last = exchanged(first)[:, None]
            late = []
        else:
            late = [blend(result[1, :half], result[0, half:]), blend(lower, result[1, half:])] + late
        lower = result[0, :half]
    late = [blend(lower, arrived)] + late
    return jnp.concatenate([exchanged(jnp.stack(late, 1)), last], 1).reshape(1, devices * owned, half * plane // devices, lanes)


def solution(mesh):
    return jax.shard_map(
        shards,
        mesh=mesh,
        in_specs=(P("az", None, "shot", None), P("az", "shot", None, None), P("az", "shot")),
        out_specs=P("az", None, "shot", None),
        check_vma=False,
    )
```

```python
import functools

import jax
import jax.numpy as jnp
import ml_dtypes
import numpy as np
from jax import lax
from jax.experimental import pallas as pl
from jax.experimental.pallas import tpu as pltpu
from jax.sharding import PartitionSpec as P


def rounded(table):
    return table.astype(ml_dtypes.bfloat16)


def real_form(real, imag):
    return np.block([[real, -imag], [imag, real]])


def dft_blocks(extent):
    n = np.arange(extent)
    phase = ((n[:, None] * n[None, :]) % extent).astype(np.float32) * np.float32(2.0 * np.pi / extent)
    scale = np.float32(extent ** (-0.5))
    cos = (np.cos(phase) * scale).astype(np.float32)
    sin = (-np.sin(phase) * scale).astype(np.float32)
    kr = np.kron(cos, cos) - np.kron(sin, sin)
    ki = np.kron(cos, sin) + np.kron(sin, cos)
    cos, sin, kr, ki = (rounded(t).astype(np.float32) for t in (cos, sin, kr, ki))
    half, plane = extent // 2, extent * extent
    eye = np.eye(extent, dtype=np.float32)
    ks = lambda t, par: t.reshape(half, 2, extent, plane)[:, par].reshape(plane // 2, plane)[:, : plane // 2]
    out = []
    for par in (0, 1):
        out.append(real_form(ks(kr, par), ks(ki, par)))
    for par in (0, 1):
        out.append(real_form(ks(kr, par).T, -ks(ki, par).T))
    for par in (0, 1):
        out.append(np.kron(real_form(cos[par::2, :half], sin[par::2, :half]), eye))
    for par in (0, 1):
        out.append(np.kron(real_form(cos[par::2, :half].T, -sin[par::2, :half].T), eye))
    return rounded(np.stack(out))


def dot(a, b):
    return jnp.dot(a, b, preferred_element_type=jnp.float32)


def patch_pair_kernel(counts_ref, obs_ref, mask_ref, table_ref, out_ref, mid, mid2, held, free, top):
    extent, plane = mask_ref.shape[1:]
    rows = obs_ref.shape[2]
    half = extent // 2
    lanes = obs_ref.shape[3]
    freq = lanes // 2
    hp = plane // 2
    count0, count1 = counts_ref[0], counts_ref[1]
    most = jnp.maximum(count0, count1)
    low_lane = lax.broadcasted_iota(jnp.int32, (plane, lanes), 1) < freq

    def observed(p, a):
        if rows >= plane:
            per = rows // plane
            block = obs_ref[a // per, p, pl.ds(pl.multiple_of(a % per * plane, plane), plane)]
        else:
            per = plane // rows
            block = obs_ref[pl.ds(a * per, per), p].reshape(plane, lanes)
        return block.astype(jnp.float32)

    def to_mid(m, xe, xo):
        for par, x in ((0, xe), (1, xo)):
            y = dot(table_ref[par], x.astype(jnp.bfloat16))
            lo, hi = y[:, :lanes], y[:, lanes:]
            for sd, v in ((0, lo + hi), (1, lo - hi)):
                v = v.astype(jnp.bfloat16).reshape(2, half, extent, lanes)
                for c in (0, 1):
                    mid[:, sd, c, m, :, par * lanes : (par + 1) * lanes] = v[c]

    def halves(x):
        a, b, c, d = x[:hp], x[hp:plane], x[plane : plane + hp], x[plane + hp :]
        return jnp.concatenate([a + b, c + d], 0), jnp.concatenate([a - b, c - d], 0)

    def begin(m, carry):
        row = lax.broadcasted_iota(jnp.int32, (2 * extent, 2 * lanes), 0)
        lane = lax.broadcasted_iota(jnp.int32, (2 * extent, 2 * lanes), 1)
        wanted = m + jnp.where(lane >= lanes, half, 0) + jnp.where(lane % lanes >= freq, extent, 0)
        pick = jnp.where(row == wanted, 1.0, 0.0).astype(jnp.bfloat16)
        marks = mask_ref[...].reshape(2 * extent, plane)
        spread = lax.dot_general(marks, pick, (((0,), (0,)), ((), ())), preferred_element_type=jnp.float32)
        free[m] = 1.0 - spread
        parts = []
        for hi in (0, 1):
            p0 = observed(0, m + hi * half)
            p1 = observed(1, m + hi * half)
            re = jnp.where(low_lane, p0, pltpu.roll(p1, freq, 1))
            im = jnp.where(low_lane, pltpu.roll(p0, freq, 1), p1)
            s = spread[:, hi * lanes : (hi + 1) * lanes]
            parts.append(jnp.concatenate([jnp.where(s > 0, re, 0.0), jnp.where(s > 0, im, 0.0)], 0))
        x = jnp.concatenate(parts, 1)
        held[m] = x.astype(jnp.bfloat16)
        xe, xo = halves(x)
        to_mid(m, xe, xo)
        return carry

    lax.fori_loop(0, half, begin, 0, unroll=8)

    def coefs(k1, sd):
        return dot(table_ref[4 + sd], mid[k1, sd].reshape(plane, 2 * lanes))

    def peak(k1, best):
        for sd in (0, 1):
            c = coefs(k1, sd)
            size = c[:hp] * c[:hp] + c[hp:] * c[hp:]
            best = jnp.maximum(best, jnp.max(size.reshape(hp // 8, 8, 2 * lanes), axis=0))
        return best

    best = lax.fori_loop(0, half, peak, jnp.zeros((8, 2 * lanes), jnp.float32), unroll=8)
    best = jnp.max(best, axis=0, keepdims=True)
    best = jnp.sqrt(jnp.maximum(best[:, :lanes], best[:, lanes:]))
    top[...] = jnp.broadcast_to(jnp.concatenate([best, best], 1) * 0.5, top.shape)

    def shrink(k1, cutoff):
        back = []
        for sd in (0, 1):
            c = coefs(k1, sd)
            re, im = c[:hp], c[hp:]
            square = jnp.maximum(re * re + im * im, 1e-30)
            size = square * lax.rsqrt(square)
            factor = jnp.maximum(size - cutoff, 0.0) * pl.reciprocal(size + 1e-6, approx=True)
            thin = jnp.concatenate([(re * factor).astype(jnp.bfloat16), (im * factor).astype(jnp.bfloat16)], 0)
            back.append(dot(table_ref[6 + sd], thin))
        for ab, v in ((0, back[0] + back[1]), (1, back[0] - back[1])):
            v = v.astype(jnp.bfloat16).reshape(2, half, extent, 2 * lanes)
            for par in (0, 1):
                for c in (0, 1):
                    mid2[:, par, c, k1, :, ab * lanes : (ab + 1) * lanes] = v[c, :, :, par * lanes : (par + 1) * lanes]
        return cutoff

    def returned(m):
        e = dot(table_ref[2], mid2[m, 0].reshape(plane, 2 * lanes))
        o = dot(table_ref[3], mid2[m, 1].reshape(plane, 2 * lanes))
        s, d = e + o, e - o
        open_ = free[m]
        obs = held[m].astype(jnp.float32)
        re = obs[:plane] + open_ * jnp.concatenate([s[:hp], d[:hp]], 0)
        im = obs[plane:] + open_ * jnp.concatenate([s[hp:], d[hp:]], 0)
        return re, im

    def again(m, carry):
        re, im = returned(m)
        xe, xo = halves(jnp.concatenate([re, im], 0))
        to_mid(m, xe, xo)
        return carry

    def sweep(k, carry):
        cutoff = top[0:1]
        lax.fori_loop(0, half, shrink, cutoff, unroll=8)
        top[...] = top[...] * 0.6
        ends0, ends1 = k == count0 - 1, k == count1 - 1

        def give(m, carry):
            re, im = returned(m)
            for hi in (0, 1):
                r, i = re[:, hi * lanes : (hi + 1) * lanes], im[:, hi * lanes : (hi + 1) * lanes]

                @pl.when(ends0)
                def _():
                    out_ref[0, m + hi * half] = jnp.where(low_lane, r, pltpu.roll(i, freq, 1)).astype(jnp.bfloat16)

                @pl.when(ends1)
                def _():
                    out_ref[1, m + hi * half] = jnp.where(low_lane, pltpu.roll(r, freq, 1), i).astype(jnp.bfloat16)

            @pl.when(k < most - 1)
            def _():
                xe, xo = halves(jnp.concatenate([re, im], 0))
                to_mid(m, xe, xo)

            return carry

        @pl.when(ends0 | ends1)
        def _():
            lax.fori_loop(0, half, give, 0, unroll=8)

        @pl.when(jnp.logical_not(ends0 | ends1))
        def _():
            lax.fori_loop(0, half, again, 0, unroll=8)

        return carry

    lax.fori_loop(0, most, sweep, 0)


def project(received, masks, sweeps, tables):
    lanes = received.shape[3]
    extent, plane = masks.shape[1:]
    half = extent // 2
    whole = pl.BlockSpec(memory_space=pltpu.VMEM)
    return pl.pallas_call(
        patch_pair_kernel,
        out_shape=jax.ShapeDtypeStruct((2, extent, plane, lanes), jnp.bfloat16),
        in_specs=[pl.BlockSpec(memory_space=pltpu.SMEM), whole, whole, whole],
        out_specs=whole,
        scratch_shapes=[
            pltpu.VMEM((half, 2, 2, half, extent, 2 * lanes), jnp.bfloat16),
            pltpu.VMEM((half, 2, 2, half, extent, 2 * lanes), jnp.bfloat16),
            pltpu.VMEM((half, 2 * plane, 2 * lanes), jnp.bfloat16),
            pltpu.VMEM((half, plane, 2 * lanes), jnp.float32),
            pltpu.VMEM((8, 2 * lanes), jnp.float32),
        ],
        compiler_params=pltpu.CompilerParams(vmem_limit_bytes=40 * 2**20),
        cost_estimate=pl.CostEstimate(flops=40 * 2**30, bytes_accessed=2**23, transcendentals=2**20),
    )(sweeps, received, masks.astype(jnp.bfloat16), tables)


def passed_along(block, axis, distance):
    devices = range(lax.axis_size(axis))
    route = [(i - distance, i) for i in devices if i - distance in devices]
    return lax.ppermute(block, axis, route)


def exchanged(parts):
    return lax.all_to_all(parts, "shot", split_axis=0, concat_axis=0, tiled=True)


def shards(spectra, sampled_mask, counts):
    devices = lax.axis_size("shot")
    owned, extent, plane = sampled_mask.shape[1:]
    rows, lanes = spectra.shape[2:]
    half = extent // 2
    tables = jnp.asarray(dft_blocks(extent))
    by_owner = spectra.reshape(devices, owned, rows, lanes)
    starts = range(owned - 2, -1, -2)
    received = []
    for s in starts:
        sent, by_owner = lax.optimization_barrier((by_owner[:, s : s + 2], by_owner))
        received.append(exchanged(sent))
    weight = ((jnp.arange(half, dtype=jnp.float32) + 0.5) / half)[:, None, None]

    def blend(own, earlier):
        mixed = weight * own.astype(jnp.float32) + (1.0 - weight) * earlier.astype(jnp.float32)
        return mixed.astype(jnp.bfloat16).reshape(devices, half * plane // devices, lanes)

    lower = None
    for i, s in enumerate(starts):
        part = received[i]
        result = project(part, sampled_mask[0, s : s + 2], counts[0, s : s + 2], tables)
        if lower is None:
            arrived = passed_along(result[1, half:], "shot", 1)
            first = blend(result[1, :half], result[0, half:])
            if len(received) > 1:
                first, received[1] = lax.optimization_barrier((first, received[1]))
            last = exchanged(first)[:, None]
            late = []
        else:
            late = [blend(result[1, :half], result[0, half:]), blend(lower, result[1, half:])] + late
        lower = result[0, :half]
    late = [blend(lower, arrived)] + late
    return jnp.concatenate([exchanged(jnp.stack(late, 1)), last], 1).reshape(1, devices * owned, half * plane // devices, lanes)


def solution(mesh):
    return jax.shard_map(
        shards,
        mesh=mesh,
        in_specs=(P("az", None, "shot", None), P("az", "shot", None, None), P("az", "shot")),
        out_specs=P("az", None, "shot", None),
        check_vma=False,
    )
```
